32 devices in a mesh: blk: 32 (over z, y, x, core), section: 1.
Axes of the slice: x: 2, y: 2, z: 4, core: 2. Of those that a mesh axis runs over, the one named last changes fastest.
Arguments:
- stream_sent: bfloat16 [1, 128, 3072], P('section', 'blk'), may hold values from -6 to 6
- grad_sent: bfloat16 [1, 128, 3072], P('section', 'blk'), may hold values from -3 to 3
- preact_now: bfloat16 [1, 128, 16384], P('section', None, 'blk'), may hold values from -6 to 6
- preact_back: bfloat16 [1, 128, 16384], P('section', None, 'blk'), may hold values from -6 to 6
- down_weight: bfloat16 [1, 16384, 3072], P('section', 'blk'), may hold values from -0.109375 to 0.109375
- block_mask: int32 [1, 128, 24], P('section', 'blk'), may hold values from 0 to 1, as said below
Outputs:
- stream_out: bfloat16 [1, 128, 3072], P('section', 'blk')
- preact_grad: bfloat16 [1, 128, 16384], P('section', None, 'blk')
- weight_grad: bfloat16 [1, 16384, 3072], P('section', 'blk')
The draws below stay inside these ranges and needn't reach their ends.
Inputs may be any that keep to these rules, and one draw needn't show every extreme that they name: `block_mask`: 1 marks a nonzero 128 x 128 block of the down projection, 0 an empty one.
All inputs are finite; a program needn't handle non-finite values.
Results may differ from the reference program's by a relative error of at most 0.005.
Values may be sent and summed in bfloat16 or wider, within the bound.
No kernel may reach another device: no remote copies, remote signals or barrier semaphores. Data moves between devices by JAX's collectives and lax.ppermute only.
A program may use at most 64 MiB of HBM per device.

```python
import jax
import jax.numpy as jnp
from jax import lax

D = 3072
FF = 16384
BLOCK = 128
SECTIONS = 1
TOKENS = 128


def draw_block_mask(key, part):
    first_key, second_key = jax.random.split(jax.random.fold_in(key, 7))
    share = jax.random.randint(first_key, (SECTIONS, FF // BLOCK, 1), 3, 30)
    drawn = jax.random.randint(second_key, (SECTIONS, FF // BLOCK, D // BLOCK), 0, 32)
    return (drawn < share).astype(jnp.int32)


def spiked(array, own_key, source, target, blocks, factor):
    owner, partner = [(jnp.arange(array.shape[axis_at]) // (array.shape[axis_at] // blocks)).reshape([-1 if axis == axis_at else 1 for axis in range(array.ndim)]) for axis_at in (source, target)]
    chosen = jax.random.permutation(own_key, blocks)[partner]
    strong = (owner == chosen) | (owner == (partner + blocks // 2) % blocks)
    return jnp.where(strong, factor * array, array)


def shard_levels(key, dims, cuts, smallest, largest):
    def one(position, shards_of):
        draws = jax.random.uniform(jax.random.fold_in(jax.random.fold_in(key, 6), position), (shards_of,), jnp.float32, smallest / len(cuts), largest / len(cuts))
        return jnp.repeat(jnp.exp(draws), dims[position] // shards_of).reshape((-1,) + (1,) * (len(dims) - position - 1))

    gain = one(*cuts[0])
    for cut in cuts[1:]:
        gain = gain * one(*cut)
    return gain


def normal_values(key, extent, spread, most, cuts=(), held_as=jnp.bfloat16):
    array = jax.random.normal(key, extent, jnp.float32) * spread
    if len(cuts) > 0:
        array = shard_levels(key, extent, cuts, -0.22, 0.18) * array
    return jnp.clip(array, min=-most, max=most).astype(held_as)


def noise_with(stream_key, extent, width, reach, cuts, heavy, held_as=jnp.bfloat16):
    values = width * jax.random.normal(stream_key, extent, jnp.float32)
    if cuts:
        values = values * shard_levels(stream_key, extent, cuts, -0.22, 0.18)
    return jnp.clip(spiked(values, jax.random.fold_in(stream_key, 3), *heavy), -reach, reach).astype(held_as)


def setup_inputs(seed: int = 0) -> dict:
    arg_keys = jax.random.split(jax.random.key(seed), 7)
    stream_sent = normal_values(arg_keys[0], (SECTIONS, TOKENS, D), 1.0, 6.0, ((1, 32),))
    grad_sent = normal_values(arg_keys[1], (SECTIONS, TOKENS, D), 0.5, 3.0, ((1, 32),))
    preact_now = noise_with(arg_keys[2], (SECTIONS, TOKENS, FF), 1.0, 6.0, ((2, 32),), (2, 1, 32, 2.75))
    preact_back = normal_values(arg_keys[3], (SECTIONS, TOKENS, FF), 1.0, 6.0, ((2, 32),))
    down_weight = normal_values(arg_keys[4], (SECTIONS, FF, D), D ** -0.5, 0.109375, ((1, 32),))
    block_mask = draw_block_mask(jax.random.fold_in(arg_keys[6], 71), 0)
    return {"stream_sent": stream_sent, "grad_sent": grad_sent, "preact_now": preact_now, "preact_back": preact_back, "down_weight": down_weight, "block_mask": block_mask}


def expand(blocks):
    values = blocks.astype(jnp.bfloat16)
    return jnp.repeat(jnp.repeat(values, BLOCK, axis=0), BLOCK, axis=1)

def one_section(pieces):
    stream, grad, preact_a, preact_b, weight, blocks = pieces
    expanded = expand(blocks)
    masked = weight * expanded
    hidden_now = jax.nn.gelu(preact_a.astype(jnp.float32)).astype(jnp.bfloat16)
    summed = jnp.dot(hidden_now, masked, preferred_element_type=jnp.float32)
    stream_out = (stream.astype(jnp.float32) + summed).astype(jnp.bfloat16)
    grad_hidden = lax.dot_general(grad, masked, (((1,), (1,)), ((), ())), preferred_element_type=jnp.float32)
    preact_f = preact_b.astype(jnp.float32)
    hidden_f, pullback = jax.vjp(jax.nn.gelu, preact_f)
    preact_grad = pullback(grad_hidden)[0].astype(jnp.bfloat16)
    hidden_back = hidden_f.astype(jnp.bfloat16)
    weight_full = lax.dot_general(hidden_back, grad, (((0,), (0,)), ((), ())), preferred_element_type=jnp.float32)
    weight_grad = (weight_full * expanded.astype(jnp.float32)).astype(jnp.bfloat16)
    return (stream_out, preact_grad, weight_grad)

def reference(stream_sent, grad_sent, preact_now, preact_back, down_weight, block_mask):
    stream = jnp.concatenate([stream_sent[:1], stream_sent[:-1]], axis=0)
    grad = jnp.concatenate([grad_sent[1:], grad_sent[-1:]], axis=0)
    stream_out, preact_grad, weight_grad = lax.map(one_section, (stream, grad, preact_now, preact_back, down_weight, block_mask))
    return (stream_out, preact_grad, weight_grad)
```

```python
import functools
import math

import jax
import jax.numpy as jnp
from jax import lax
from jax.experimental import pallas as pl
from jax.experimental.pallas import tpu as pltpu
from jax.sharding import PartitionSpec as P

BLOCK = 128
SCALE = math.sqrt(2.0 / math.pi)
CUBIC = 0.044715
CHUNK = 512
bf16 = jnp.bfloat16
f32 = jnp.float32


def shifted(block, axis, distance):
    devices = range(lax.axis_size(axis))
    route = [(i - distance, i) for i in devices if i - distance in devices]
    return lax.ppermute(block, axis, route)


def exchange(block, bit):
    return lax.ppermute(block, "blk", [(i, i ^ bit) for i in range(lax.axis_size("blk"))])


def own_token(place, me, order, each):
    group, within = place // each, place % each
    owner = me
    for k, bit in enumerate(order):
        owner = owner ^ jnp.where((group >> (len(order) - 1 - k)) & 1 == 1, bit, 0)
    return owner * each + within


def reorder(me, tokens, order, back=False):
    rows = lax.broadcasted_iota(jnp.int32, (tokens, tokens), 1 if back else 0)
    cols = lax.broadcasted_iota(jnp.int32, (tokens, tokens), 0 if back else 1)
    return (own_token(rows, me, order, tokens >> len(order)) == cols).astype(bf16)


def masked_block(w_ref, mask_ref, first):
    rows = []
    for i in range(w_ref.shape[0] // BLOCK):
        row = []
        for j in range(w_ref.shape[1] // BLOCK):
            block = w_ref[i * BLOCK : (i + 1) * BLOCK, j * BLOCK : (j + 1) * BLOCK]
            row.append(jnp.where(mask_ref[i, first + j] != 0, block, jnp.zeros_like(block)))
        rows.append(jnp.concatenate(row, axis=1))
    return jnp.concatenate(rows, axis=0)


def forward_kernel(order, me_ref, mask_ref, pre_ref, w_ref, keep_ref, send_ref, hidden_ref):
    step = pl.program_id(0)
    tokens = pre_ref.shape[0]

    @pl.when(step == 0)
    def _():
        x = pre_ref[...].astype(f32)
        hidden = 0.5 * x * (1.0 + jnp.tanh(SCALE * (x + CUBIC * x * x * x)))
        moved = jnp.dot(reorder(me_ref[0], tokens, order), hidden.astype(bf16), preferred_element_type=f32)
        hidden_ref[...] = moved.astype(bf16)

    masked = masked_block(w_ref, mask_ref, step * (w_ref.shape[1] // BLOCK))
    product = jnp.dot(hidden_ref[...], masked, preferred_element_type=f32)
    keep_ref[...] = product[: tokens // 2]
    send_ref[...] = product[tokens // 2 :].astype(bf16)


def prepare_kernel(order, me_ref, pre_ref, hidden_ref, slope_ref):
    tokens = pre_ref.shape[0]
    moved = jnp.dot(reorder(me_ref[0], tokens, order), pre_ref[...], preferred_element_type=f32)
    square = moved * moved
    t = jnp.tanh(SCALE * (moved + CUBIC * moved * square))
    half = 0.5 * (1.0 + t)
    hidden_ref[...] = (moved * half).astype(bf16)
    slope_ref[...] = half + 0.5 * moved * (1.0 - t * t) * (SCALE * (1.0 + 3.0 * CUBIC * square))


def backward_kernel(order, me_ref, mask_ref, mine_ref, other_ref, w_ref, hidden_ref, slope_ref, wg_ref, pg_ref, acc_ref):
    step = pl.program_id(0)
    first = step * (w_ref.shape[1] // BLOCK)
    grad = jnp.concatenate([mine_ref[...], other_ref[...]], axis=0)
    masked = masked_block(w_ref, mask_ref, first)
    part = lax.dot_general(grad, masked, (((1,), (1,)), ((), ())), preferred_element_type=f32)

    @pl.when(step == 0)
    def _():
        acc_ref[...] = part

    @pl.when(step > 0)
    def _():
        acc_ref[...] += part

    full = lax.dot_general(hidden_ref[...], grad, (((0,), (0,)), ((), ())), preferred_element_type=f32)
    for i in range(w_ref.shape[0] // BLOCK):
        for j in range(w_ref.shape[1] // BLOCK):
            block = full[i * BLOCK : (i + 1) * BLOCK, j * BLOCK : (j + 1) * BLOCK]
            kept = jnp.where(mask_ref[i, first + j] != 0, block, jnp.zeros_like(block))
            wg_ref[i * BLOCK : (i + 1) * BLOCK, j * BLOCK : (j + 1) * BLOCK] = kept.astype(bf16)

    @pl.when(step == pl.num_programs(0) - 1)
    def _():
        tokens = pg_ref.shape[0]
        moved = (acc_ref[...] * slope_ref[...]).astype(bf16)
        back = reorder(me_ref[0], tokens, order, back=True)
        pg_ref[...] = jnp.dot(back, moved, preferred_element_type=f32).astype(bf16)


SMEM = functools.partial(pl.BlockSpec, memory_space=pltpu.SMEM)


def body(stream_sent, grad_sent, preact_now, preact_back, down_weight, block_mask):
    sections = lax.axis_size("section")
    stream, grad = stream_sent, grad_sent
    if sections > 1:
        section_index = lax.axis_index("section")
        stream = jnp.where(section_index == 0, stream, shifted(stream, "section", 1))
        grad = jnp.where(section_index == sections - 1, grad, shifted(grad, "section", -1))
    stream, grad, mask, weight = stream[0], grad[0], block_mask[0], down_weight[0]
    pre_now, pre_back = preact_now[0], preact_back[0]
    tokens, hidden = pre_now.shape
    width = weight.shape[1]
    chunk = CHUNK if width % CHUNK == 0 else BLOCK
    devices = lax.axis_size("blk")
    order = [1 << k for k in range(devices.bit_length() - 1)]
    me = lax.axis_index("blk").astype(jnp.int32).reshape(1)

    def whole(rows, cols):
        return pl.BlockSpec((rows, cols), lambda c: (0, 0))

    def column(rows):
        return pl.BlockSpec((rows, chunk), lambda c: (0, c))

    half = tokens // 2
    keep, send = pl.pallas_call(
        functools.partial(forward_kernel, order),
        grid=(width // chunk,),
        out_shape=(jax.ShapeDtypeStruct((half, width), f32), jax.ShapeDtypeStruct((half, width), bf16)),
        in_specs=[SMEM(), SMEM(), whole(tokens, hidden), column(hidden)],
        out_specs=(column(half), column(half)),
        scratch_shapes=[pltpu.VMEM((tokens, hidden), bf16)],
        cost_estimate=pl.CostEstimate(flops=2 * tokens * hidden * width, bytes_accessed=2 * hidden * width, transcendentals=0),
        name="forward",
    )(me, mask, pre_now, weight)

    hidden_back, slope = pl.pallas_call(
        functools.partial(prepare_kernel, order),
        out_shape=(jax.ShapeDtypeStruct((tokens, hidden), bf16), jax.ShapeDtypeStruct((tokens, hidden), f32)),
        in_specs=[SMEM(), pl.BlockSpec(memory_space=pltpu.VMEM)],
        name="prepare",
    )(me, pre_back)

    mine = grad
    for bit in order[:0:-1]:
        mine = jnp.concatenate([mine, exchange(mine, bit)], axis=0)
    other = exchange(mine, order[0])

    for bit in order:
        total = keep + exchange(send, bit).astype(f32)
        rows = total.shape[0] // 2
        keep, send = total[:rows], total[rows:].astype(bf16)
    stream_out = (stream.astype(f32) + total).astype(bf16)

    weight_grad, preact_grad = pl.pallas_call(
        functools.partial(backward_kernel, order),
        grid=(width // chunk,),
        out_shape=(jax.ShapeDtypeStruct((hidden, width), bf16), jax.ShapeDtypeStruct((tokens, hidden), bf16)),
        in_specs=[SMEM(), SMEM(), column(half), column(half), column(hidden), whole(tokens, hidden), whole(tokens, hidden)],
        out_specs=(column(hidden), whole(tokens, hidden)),
        scratch_shapes=[pltpu.VMEM((tokens, hidden), f32)],
        cost_estimate=pl.CostEstimate(flops=4 * tokens * hidden * width, bytes_accessed=4 * hidden * width, transcendentals=0),
        name="backward",
    )(me, mask, mine, other, weight, hidden_back, slope)
    return stream_out[None], preact_grad[None], weight_grad[None]


def solution(mesh):
    placed = (
        P("section", "blk", None),
        P("section", "blk", None),
        P("section", None, "blk"),
        P("section", None, "blk"),
        P("section", "blk", None),
        P("section", "blk", None),
    )
    return jax.shard_map(
        body,
        mesh=mesh,
        in_specs=placed,
        out_specs=(P("section", "blk", None), P("section", None, "blk"), P("section", "blk", None)),
        check_vma=False,
    )
```

```python
import functools
import math

import jax
import jax.numpy as jnp
from jax import lax
from jax.experimental import pallas as pl
from jax.experimental.pallas import tpu as pltpu
from jax.sharding import PartitionSpec as P

BLOCK = 128
SCALE = math.sqrt(2.0 / math.pi)
CUBIC = 0.044715
CHUNK = 512
LIMIT = 16 * 1024 * 1024
SEND_BYTES = 6_000_000
KEEP_BYTES = 3_000_000
bf16 = jnp.bfloat16
f32 = jnp.float32


def shifted(block, axis, distance):
    devices = range(lax.axis_size(axis))
    route = [(i - distance, i) for i in devices if i - distance in devices]
    return lax.ppermute(block, axis, route)


def exchange(block, bit):
    return lax.ppermute(block, "blk", [(i, i ^ bit) for i in range(lax.axis_size("blk"))])


def combinations(bits):
    found = [0]
    for bit in bits[::-1]:
        found += [bit ^ other for other in found]
    return found


def own_token(place, me, order, each):
    group, within = place // each, place % each
    owner = me
    for k, bit in enumerate(order):
        owner = owner ^ jnp.where((group >> (len(order) - 1 - k)) & 1 == 1, bit, 0)
    return owner * each + within


def reorder(me, tokens, order, back=False):
    rows = lax.broadcasted_iota(jnp.int32, (tokens, tokens), 1 if back else 0)
    cols = lax.broadcasted_iota(jnp.int32, (tokens, tokens), 0 if back else 1)
    return (own_token(rows, me, order, tokens >> len(order)) == cols).astype(bf16)


def columns(width):
    chunk = CHUNK if width % CHUNK == 0 else BLOCK
    return [pl.ds(first, chunk) for first in range(0, width, chunk)]


def keep_blocks(array, mask_ref, i, first):
    blocks = []
    for j in range(array.shape[1] // BLOCK):
        block = array[:, j * BLOCK : (j + 1) * BLOCK]
        blocks.append(jnp.where(mask_ref[i, first + j] != 0, block, jnp.zeros_like(block)))
    return jnp.concatenate(blocks, axis=1)


def gelu_and_slope(x):
    square = x * x
    t = jnp.tanh(SCALE * (x + CUBIC * x * square))
    half = 0.5 * (1.0 + t)
    slope = half + 0.5 * x * (1.0 - t * t) * (SCALE * (1.0 + 3.0 * CUBIC * square))
    return x * half, slope


def send_kernel(
    order, me_ref, mask_hbm, now_hbm, back_hbm, w_hbm, send_ref, hidden_ref, masked_ref, back_ref, mask_ref, now_ref, w_ref, sems
):
    bands = w_ref.shape[0] // BLOCK
    pairs = [(now_hbm, now_ref), (mask_hbm, mask_ref)]
    pairs += [(w_hbm.at[pl.ds(i * BLOCK, BLOCK)], w_ref.at[pl.ds(i * BLOCK, BLOCK)]) for i in range(bands)]
    pairs += [(back_hbm, back_ref)]
    copies = [pltpu.make_async_copy(source, target, sems.at[k]) for k, (source, target) in enumerate(pairs)]
    for copy in copies:
        copy.start()
    tokens = now_ref.shape[0]
    moves = reorder(me_ref[0], tokens, order)
    copies[0].wait()
    hidden, _ = gelu_and_slope(jnp.dot(moves, now_ref[...], preferred_element_type=f32))
    hidden_ref[...] = hidden.astype(bf16)
    copies[1].wait()
    for i in range(bands):
        copies[2 + i].wait()
        rows = pl.ds(i * BLOCK, BLOCK)
        masked_ref[rows] = keep_blocks(w_ref[rows], mask_ref, i, 0)
    half = send_ref.shape[0]
    for part in columns(w_ref.shape[1]):
        product = jnp.dot(hidden_ref[half:], masked_ref[:, part], preferred_element_type=f32)
        send_ref[:, part] = product.astype(bf16)
    copies[-1].wait()


def keep_kernel(order, me_ref, hidden_now_ref, masked_ref, back_ref, keep_ref, hidden_ref, slope_ref):
    half = keep_ref.shape[0]
    for part in columns(masked_ref.shape[1]):
        keep_ref[:, part] = jnp.dot(hidden_now_ref[:half], masked_ref[:, part], preferred_element_type=f32)
    moves = reorder(me_ref[0], back_ref.shape[0], order)
    hidden, slope = gelu_and_slope(jnp.dot(moves, back_ref[...], preferred_element_type=f32))
    hidden_ref[...] = hidden.astype(bf16)
    slope_ref[...] = slope


def backward_kernel(order, pieces, me_ref, mask_ref, *refs):
    grads = refs[:pieces]
    w_ref, hidden_ref, slope_ref, wg_hbm, pg_ref, wg_ref, sems = refs[pieces:]
    tokens = pg_ref.shape[0]
    results = []
    total = jnp.zeros((tokens, w_ref.shape[0]), f32)
    for c, part in enumerate(columns(w_ref.shape[1])):
        grad = jnp.concatenate([g[:, part] for g in grads], axis=0)
        full = lax.dot_general(hidden_ref[...], grad, (((0,), (0,)), ((), ())), preferred_element_type=f32)
        for i in range(w_ref.shape[0] // BLOCK):
            rows = pl.ds(i * BLOCK, BLOCK)
            wg_ref[rows, part] = keep_blocks(full[i * BLOCK : (i + 1) * BLOCK], mask_ref, i, part.start // BLOCK).astype(bf16)
        result = pltpu.make_async_copy(wg_ref.at[:, part], wg_hbm.at[:, part], sems.at[c])
        result.start()
        results.append(result)
        total += lax.dot_general(grad, w_ref[:, part], (((1,), (1,)), ((), ())), preferred_element_type=f32)
    moved = (total * slope_ref[...]).astype(bf16)
    back = reorder(me_ref[0], tokens, order, back=True)
    pg_ref[...] = jnp.dot(back, moved, preferred_element_type=f32).astype(bf16)
    for result in results:
        result.wait()


SMEM = functools.partial(pl.BlockSpec, memory_space=pltpu.SMEM)
VMEM = functools.partial(pl.BlockSpec, memory_space=pltpu.VMEM)
HBM = functools.partial(pl.BlockSpec, memory_space=pltpu.HBM)


def body(stream_sent, grad_sent, preact_now, preact_back, down_weight, block_mask):
    sections = lax.axis_size("section")
    stream, grad = stream_sent, grad_sent
    if sections > 1:
        section_index = lax.axis_index("section")
        stream = jnp.where(section_index == 0, stream, shifted(stream, "section", 1))
        grad = jnp.where(section_index == sections - 1, grad, shifted(grad, "section", -1))
    stream, grad, mask, weight = stream[0], grad[0], block_mask[0], down_weight[0]
    pre_now, pre_back = preact_now[0], preact_back[0]
    held = [pltpu.with_memory_space_constraint(x, pltpu.HBM) for x in (mask, pre_now, pre_back, weight)]
    tokens, hidden = preact_now.shape[1:]
    width = down_weight.shape[2]
    devices = lax.axis_size("blk")
    bits = [1 << k for k in range(devices.bit_length() - 1)]
    near, plane, far = bits[:1], bits[1:3], bits[3:]
    scatter_order = near + plane + far
    gather_order = near + plane + far[::-1]
    me = lax.axis_index("blk").astype(jnp.int32).reshape(1)
    chunks = len(columns(width))
    half = tokens // 2

    def shape(dtype, *dims):
        return jax.ShapeDtypeStruct(dims, dtype)

    params = pltpu.CompilerParams(vmem_limit_bytes=LIMIT)
    send, hidden_now, masked, held_back = pl.pallas_call(
        functools.partial(send_kernel, scatter_order),
        out_shape=(shape(bf16, half, width), shape(bf16, tokens, hidden), shape(bf16, hidden, width), shape(bf16, tokens, hidden)),
        in_specs=[SMEM()] + [HBM()] * 4,
        out_specs=(VMEM(),) * 4,
        scratch_shapes=[
            pltpu.SMEM(mask.shape, jnp.int32),
            pltpu.VMEM((tokens, hidden), bf16),
            pltpu.VMEM((hidden, width), bf16),
            pltpu.SemaphoreType.DMA((3 + hidden // BLOCK,)),
        ],
        compiler_params=params,
        cost_estimate=pl.CostEstimate(flops=tokens * hidden * width, bytes_accessed=SEND_BYTES, transcendentals=0),
        name="send",
    )(me, *held)

    mine = grad
    for k, bit in enumerate(far):
        other = exchange(mine, bit)
        if k == 0:
            send, other = lax.optimization_barrier((send, other))
        mine = jnp.concatenate([mine, other], axis=0)

    keep, hidden_back, slope = pl.pallas_call(
        functools.partial(keep_kernel, gather_order),
        out_shape=(shape(f32, half, width), shape(bf16, tokens, hidden), shape(f32, tokens, hidden)),
        in_specs=[SMEM()] + [VMEM()] * 3,
        out_specs=(VMEM(),) * 3,
        compiler_params=params,
        cost_estimate=pl.CostEstimate(flops=tokens * hidden * width, bytes_accessed=KEEP_BYTES, transcendentals=0),
        name="keep",
    )(me, hidden_now, masked, held_back)

    total = keep + exchange(send, near[0]).astype(f32)
    for group in [plane] + [[bit] for bit in far]:
        masks = combinations(group)
        parts = jnp.split(total, len(masks), axis=0)
        total = parts[0]
        for part, bit in zip(parts[1:], masks[1:]):
            total = total + exchange(part.astype(bf16), bit).astype(f32)
    stream_out = (stream.astype(f32) + total).astype(bf16)

    grads = [mine] + [exchange(mine, bit) for bit in combinations(plane)[1:]]
    grads += [exchange(piece, near[0]) for piece in grads]

    weight_grad, preact_grad = pl.pallas_call(
        functools.partial(backward_kernel, gather_order, len(grads)),
        out_shape=(jax.ShapeDtypeStruct((hidden, width), bf16), jax.ShapeDtypeStruct((tokens, hidden), bf16)),
        in_specs=[SMEM(), SMEM()] + [VMEM()] * (len(grads) + 3),
        out_specs=(HBM(), VMEM()),
        scratch_shapes=[
            pltpu.VMEM((hidden, width), bf16),
            pltpu.SemaphoreType.DMA((chunks,)),
        ],
        compiler_params=params,
        cost_estimate=pl.CostEstimate(flops=4 * tokens * hidden * width, bytes_accessed=4 * hidden * width, transcendentals=0),
        name="backward",
    )(me, mask, *grads, masked, hidden_back, slope)
    return stream_out[None], preact_grad[None], weight_grad[None]


def solution(mesh):
    placed = (
        P("section", "blk", None),
        P("section", "blk", None),
        P("section", None, "blk"),
        P("section", None, "blk"),
        P("section", "blk", None),
        P("section", "blk", None),
    )
    return jax.shard_map(
        body,
        mesh=mesh,
        in_specs=placed,
        out_specs=(P("section", "blk", None), P("section", None, "blk"), P("section", "blk", None)),
        check_vma=False,
    )
```

```python
import functools
import math

import jax
import jax.numpy as jnp
from jax import lax
from jax.experimental import pallas as pl
from jax.experimental.pallas import tpu as pltpu
from jax.sharding import PartitionSpec as P

BLOCK = 128
SCALE = math.sqrt(2.0 / math.pi)
CUBIC = 0.044715
CHUNK = 512
WIDE = 1024
LIMIT = 16 * 1024 * 1024
FORWARD_BYTES = 6_000_000
PREPARE_BYTES = 1_500_000
bf16 = jnp.bfloat16
f32 = jnp.float32


def shifted(block, axis, distance):
    devices = range(lax.axis_size(axis))
    route = [(i - distance, i) for i in devices if i - distance in devices]
    return lax.ppermute(block, axis, route)


def exchange(block, bit):
    return lax.ppermute(block, "blk", [(i, i ^ bit) for i in range(lax.axis_size("blk"))])


def combinations(bits):
    found = [0]
    for bit in bits[::-1]:
        found += [bit ^ other for other in found]
    return found


def own_token(place, me, order, each):
    group, within = place // each, place % each
    owner = me
    for k, bit in enumerate(order):
        owner = owner ^ jnp.where((group >> (len(order) - 1 - k)) & 1 == 1, bit, 0)
    return owner * each + within


def reorder(me, tokens, order, back=False):
    rows = lax.broadcasted_iota(jnp.int32, (tokens, tokens), 1 if back else 0)
    cols = lax.broadcasted_iota(jnp.int32, (tokens, tokens), 0 if back else 1)
    return (own_token(rows, me, order, tokens >> len(order)) == cols).astype(bf16)


def columns(width, chunk):
    chunk = chunk if width % chunk == 0 else BLOCK
    return [pl.ds(first, chunk) for first in range(0, width, chunk)]


def keep_blocks(array, mask_ref, i, first):
    blocks = []
    for j in range(array.shape[1] // BLOCK):
        block = array[:, j * BLOCK : (j + 1) * BLOCK]
        blocks.append(jnp.where(mask_ref[i, first + j] != 0, block, jnp.zeros_like(block)))
    return jnp.concatenate(blocks, axis=1)


def gelu_and_slope(x):
    square = x * x
    t = jnp.tanh(SCALE * (x + CUBIC * x * square))
    half = 0.5 * (1.0 + t)
    slope = half + 0.5 * x * (1.0 - t * t) * (SCALE * (1.0 + 3.0 * CUBIC * square))
    return x * half, slope


def forward_kernel(order, me_ref, mask_hbm, now_hbm, back_hbm, w_hbm, *refs):
    total_ref, send_ref, masked_ref, kept_ref, back_ref, mask_ref, now_ref, w_ref, sems = refs
    parts = columns(w_ref.shape[1], WIDE)
    pairs = [(now_hbm, now_ref), (mask_hbm, mask_ref)]
    pairs += [(w_hbm.at[:, part], w_ref.at[:, part]) for part in parts]
    pairs += [(back_hbm, back_ref)]
    copies = [pltpu.make_async_copy(source, target, sems.at[k]) for k, (source, target) in enumerate(pairs)]
    for copy in copies:
        copy.start()
    tokens = now_ref.shape[0]
    half = send_ref.shape[0]
    moves = reorder(me_ref[0], tokens, order)
    copies[0].wait()
    hidden = gelu_and_slope(jnp.dot(moves, now_ref[...], preferred_element_type=f32))[0].astype(bf16)
    copies[1].wait()
    for i in range(w_ref.shape[0] // BLOCK):
        for j in range(w_ref.shape[1] // BLOCK):
            kept_ref[i : i + 1, j * BLOCK : (j + 1) * BLOCK] = jnp.where(mask_ref[i, j] != 0, jnp.ones((1, BLOCK), f32), 0.0)
    for c, part in enumerate(parts):
        copies[2 + c].wait()
        for i in range(w_ref.shape[0] // BLOCK):
            rows = pl.ds(i * BLOCK, BLOCK)
            masked_ref[rows, part] = keep_blocks(w_ref[rows, part], mask_ref, i, part.start // BLOCK)
        product = jnp.dot(hidden, masked_ref[:, part], preferred_element_type=f32)
        total_ref[:, part] = product[:half]
        send_ref[:, part] = product[half:].astype(bf16)
    copies[-1].wait()


def prepare_kernel(order, me_ref, back_ref, hidden_ref, slope_ref):
    moves = reorder(me_ref[0], back_ref.shape[0], order, back=True)
    hidden, slope = gelu_and_slope(jnp.dot(back_ref[...].T, moves, preferred_element_type=f32))
    hidden_ref[...] = hidden.astype(bf16)
    slope_ref[...] = slope


def backward_kernel(order, pieces, me_ref, *refs):
    grads = refs[:pieces]
    kept_ref, w_ref, hidden_ref, slope_ref, wg_hbm, pg_hbm, grad_ref, wg_ref, pg_ref, sems = refs[pieces:]
    tokens = pg_ref.shape[0]
    parts = columns(w_ref.shape[1], CHUNK)
    results = []
    for c, part in enumerate(parts):
        for k, piece in enumerate(grads):
            rows = piece.shape[0]
            grad_ref[k * rows : (k + 1) * rows, part] = piece[:, part]
        full = jnp.dot(hidden_ref[...], grad_ref[:, part], preferred_element_type=f32)
        for i in range(w_ref.shape[0] // BLOCK):
            band = full[i * BLOCK : (i + 1) * BLOCK] * kept_ref[i : i + 1, part]
            wg_ref[pl.ds(i * BLOCK, BLOCK), part] = band.astype(bf16)
        results.append(pltpu.make_async_copy(wg_ref.at[:, part], wg_hbm.at[:, part], sems.at[c]))
        results[-1].start()
    total = lax.dot_general(w_ref[...], grad_ref[...], (((1,), (1,)), ((), ())), preferred_element_type=f32)
    moved = (total * slope_ref[...]).astype(bf16)
    back = reorder(me_ref[0], tokens, order, back=True)
    pg_ref[...] = lax.dot_general(back, moved, (((1,), (1,)), ((), ())), preferred_element_type=f32).astype(bf16)
    results.append(pltpu.make_async_copy(pg_ref, pg_hbm, sems.at[len(parts)]))
    results[-1].start()
    for result in results:
        result.wait()


SMEM = functools.partial(pl.BlockSpec, memory_space=pltpu.SMEM)
VMEM = functools.partial(pl.BlockSpec, memory_space=pltpu.VMEM)
HBM = functools.partial(pl.BlockSpec, memory_space=pltpu.HBM)


def body(stream_sent, grad_sent, preact_now, preact_back, down_weight, block_mask):
    sections = lax.axis_size("section")
    stream, grad = stream_sent, grad_sent
    if sections > 1:
        section_index = lax.axis_index("section")
        stream = jnp.where(section_index == 0, stream, shifted(stream, "section", 1))
        grad = jnp.where(section_index == sections - 1, grad, shifted(grad, "section", -1))
    stream, grad, mask, weight = stream[0], grad[0], block_mask[0], down_weight[0]
    pre_now, pre_back = preact_now[0], preact_back[0]
    held = [pltpu.with_memory_space_constraint(x, pltpu.HBM) for x in (mask, pre_now, pre_back, weight)]
    tokens, hidden = preact_now.shape[1:]
    width = down_weight.shape[2]
    devices = lax.axis_size("blk")
    bits = [1 << k for k in range(devices.bit_length() - 1)]
    near, plane, far = bits[:1], bits[1:3], bits[3:]
    scatter_order = near + plane + far
    gather_order = near + plane + far[::-1]
    me = lax.axis_index("blk").astype(jnp.int32).reshape(1)
    half = tokens // 2

    def shape(dtype, *dims):
        return jax.ShapeDtypeStruct(dims, dtype)

    params = pltpu.CompilerParams(vmem_limit_bytes=LIMIT)
    total, send, masked, kept, held_back = pl.pallas_call(
        functools.partial(forward_kernel, scatter_order),
        out_shape=(
            shape(f32, half, width),
            shape(bf16, half, width),
            shape(bf16, hidden, width),
            shape(f32, hidden // BLOCK, width),
            shape(bf16, tokens, hidden),
        ),
        in_specs=[SMEM()] + [HBM()] * 4,
        out_specs=(VMEM(),) * 5,
        scratch_shapes=[
            pltpu.SMEM(mask.shape, jnp.int32),
            pltpu.VMEM((tokens, hidden), bf16),
            pltpu.VMEM((hidden, width), bf16),
            pltpu.SemaphoreType.DMA((3 + len(columns(width, WIDE)),)),
        ],
        compiler_params=params,
        cost_estimate=pl.CostEstimate(flops=2 * tokens * hidden * width, bytes_accessed=FORWARD_BYTES, transcendentals=0),
        name="forward",
    )(me, *held)

    hidden_back, slope = pl.pallas_call(
        functools.partial(prepare_kernel, gather_order),
        out_shape=(shape(bf16, hidden, tokens), shape(f32, hidden, tokens)),
        in_specs=[SMEM(), VMEM()],
        out_specs=(VMEM(),) * 2,
        compiler_params=params,
        cost_estimate=pl.CostEstimate(flops=2 * tokens * tokens * hidden, bytes_accessed=PREPARE_BYTES, transcendentals=0),
        name="prepare",
    )(me, held_back)

    mine = grad
    for k, bit in enumerate(far):
        other = exchange(mine, bit)
        if k == 0:
            send, other = lax.optimization_barrier((send, other))
        mine = jnp.concatenate([mine, other], axis=0)

    total = total + exchange(send, near[0]).astype(f32)
    parts = jnp.split(total, 1 << len(plane), axis=0)
    total = parts[0]
    for part, bit in zip(parts[1:], combinations(plane)[1:]):
        total = total + exchange(part.astype(bf16), bit).astype(f32)
    for bit in far:
        part = total[total.shape[0] // 2 :].astype(bf16)
        total = total[: total.shape[0] // 2]
        if bit == far[-1]:
            total = total + stream.astype(f32)
        total = total + exchange(part, bit).astype(f32)
    stream_out = total.astype(bf16)

    grads = [mine] + [exchange(mine, bit) for bit in combinations(plane)[1:]]
    grads += [exchange(piece, near[0]) for piece in grads]

    weight_grad, preact_grad = pl.pallas_call(
        functools.partial(backward_kernel, gather_order, len(grads)),
        out_shape=(shape(bf16, hidden, width), shape(bf16, tokens, hidden)),
        in_specs=[SMEM()] + [VMEM()] * (len(grads) + 4),
        out_specs=(HBM(), HBM()),
        scratch_shapes=[
            pltpu.VMEM((tokens, width), bf16),
            pltpu.VMEM((hidden, width), bf16),
            pltpu.VMEM((tokens, hidden), bf16),
            pltpu.SemaphoreType.DMA((1 + len(columns(width, CHUNK)),)),
        ],
        compiler_params=params,
        cost_estimate=pl.CostEstimate(flops=4 * tokens * hidden * width, bytes_accessed=4 * hidden * width, transcendentals=0),
        name="backward",
    )(me, *grads, kept, masked, hidden_back, slope)
    return stream_out[None], preact_grad[None], weight_grad[None]


def solution(mesh):
    placed = (
        P("section", "blk", None),
        P("section", "blk", None),
        P("section", None, "blk"),
        P("section", None, "blk"),
        P("section", "blk", None),
        P("section", "blk", None),
    )
    return jax.shard_map(
        body,
        mesh=mesh,
        in_specs=placed,
        out_specs=(P("section", "blk", None), P("section", None, "blk"), P("section", "blk", None)),
        check_vma=False,
    )
```

```python
import functools
import math

import jax
import jax.numpy as jnp
from jax import lax
from jax.experimental import pallas as pl
from jax.experimental.pallas import tpu as pltpu
from jax.sharding import PartitionSpec as P

BLOCK = 128
SCALE = math.sqrt(2.0 / math.pi)
CUBIC = 0.044715
CHUNK = 512
WIDE = 1024
LIMIT = 16 * 1024 * 1024
FORWARD_BYTES = 6_000_000
PREPARE_BYTES = 1_500_000
bf16 = jnp.bfloat16
f32 = jnp.float32


def shifted(block, axis, distance):
    devices = range(lax.axis_size(axis))
    route = [(i - distance, i) for i in devices if i - distance in devices]
    return lax.ppermute(block, axis, route)


def exchange(block, bit):
    return lax.ppermute(block, "blk", [(i, i ^ bit) for i in range(lax.axis_size("blk"))])


def combinations(bits):
    found = [0]
    for bit in bits[::-1]:
        found += [bit ^ other for other in found]
    return found


def own_token(place, me, order, each):
    group, within = place // each, place % each
    owner = me
    for k, bit in enumerate(order):
        owner = owner ^ jnp.where((group >> (len(order) - 1 - k)) & 1 == 1, bit, 0)
    return owner * each + within


def reorder(me, tokens, order, back=False):
    rows = lax.broadcasted_iota(jnp.int32, (tokens, tokens), 1 if back else 0)
    cols = lax.broadcasted_iota(jnp.int32, (tokens, tokens), 0 if back else 1)
    return (own_token(rows, me, order, tokens >> len(order)) == cols).astype(bf16)


def columns(width, chunk):
    chunk = chunk if width % chunk == 0 else BLOCK
    return [pl.ds(first, chunk) for first in range(0, width, chunk)]


def keep_blocks(array, mask_ref, i, first):
    blocks = []
    for j in range(array.shape[1] // BLOCK):
        block = array[:, j * BLOCK : (j + 1) * BLOCK]
        blocks.append(jnp.where(mask_ref[i, first + j] != 0, block, jnp.zeros_like(block)))
    return jnp.concatenate(blocks, axis=1)


def gelu_and_slope(x):
    square = x * x
    t = jnp.tanh(SCALE * (x + CUBIC * x * square))
    half = 0.5 * (1.0 + t)
    slope = half + 0.5 * x * (1.0 - t * t) * (SCALE * (1.0 + 3.0 * CUBIC * square))
    return x * half, slope


def forward_kernel(order, me_ref, mask_hbm, now_hbm, back_hbm, w_hbm, *refs):
    total_ref, send_ref, masked_ref, kept_ref, back_ref, mask_ref, now_ref, w_ref, sems = refs
    parts = columns(w_ref.shape[1], WIDE)
    pairs = [(now_hbm, now_ref), (mask_hbm, mask_ref)]
    pairs += [(w_hbm.at[:, part], w_ref.at[:, part]) for part in parts]
    pairs += [(back_hbm, back_ref)]
    copies = [pltpu.make_async_copy(source, target, sems.at[k]) for k, (source, target) in enumerate(pairs)]
    for copy in copies:
        copy.start()
    tokens = now_ref.shape[0]
    half = send_ref.shape[0]
    moves = reorder(me_ref[0], tokens, order)
    copies[0].wait()
    hidden = gelu_and_slope(jnp.dot(moves, now_ref[...], preferred_element_type=f32))[0].astype(bf16)
    copies[1].wait()
    for i in range(w_ref.shape[0] // BLOCK):
        for j in range(w_ref.shape[1] // BLOCK):
            kept_ref[i : i + 1, j * BLOCK : (j + 1) * BLOCK] = jnp.where(mask_ref[i, j] != 0, jnp.ones((1, BLOCK), f32), 0.0)
    for c, part in enumerate(parts):
        copies[2 + c].wait()
        for i in range(w_ref.shape[0] // BLOCK):
            rows = pl.ds(i * BLOCK, BLOCK)
            masked_ref[rows, part] = keep_blocks(w_ref[rows, part], mask_ref, i, part.start // BLOCK)
        product = jnp.dot(hidden, masked_ref[:, part], preferred_element_type=f32)
        total_ref[:, part] = product[:half]
        send_ref[:, part] = product[half:].astype(bf16)
    copies[-1].wait()


def prepare_kernel(order, me_ref, back_ref, hidden_ref, slope_ref):
    moves = reorder(me_ref[0], back_ref.shape[0], order, back=True)
    hidden, slope = gelu_and_slope(jnp.dot(back_ref[...].T, moves, preferred_element_type=f32))
    hidden_ref[...] = hidden.astype(bf16)
    slope_ref[...] = slope


def pack_kernel(places, *refs):
    *pieces, out_ref = refs
    for k, piece in zip(places, pieces):
        rows = piece.shape[0]
        out_ref[k * rows : (k + 1) * rows] = piece[...]


def backward_kernel(order, pieces, me_ref, *refs):
    grads = refs[:pieces]
    kept_ref, w_ref, hidden_ref, slope_ref, wg_hbm, pg_hbm, grad_ref, wg_ref, pg_ref, sems = refs[pieces:]
    tokens = pg_ref.shape[0]
    parts = columns(w_ref.shape[1], CHUNK)
    results = []
    for c, part in enumerate(parts):
        for k, piece in enumerate(grads):
            rows = piece.shape[0]
            grad_ref[k * rows : (k + 1) * rows, part] = piece[:, part]
        full = jnp.dot(hidden_ref[...], grad_ref[:, part], preferred_element_type=f32)
        for i in range(w_ref.shape[0] // BLOCK):
            band = full[i * BLOCK : (i + 1) * BLOCK] * kept_ref[i : i + 1, part]
            wg_ref[pl.ds(i * BLOCK, BLOCK), part] = band.astype(bf16)
        results.append(pltpu.make_async_copy(wg_ref.at[:, part], wg_hbm.at[:, part], sems.at[c]))
        results[-1].start()
    total = lax.dot_general(w_ref[...], grad_ref[...], (((1,), (1,)), ((), ())), preferred_element_type=f32)
    moved = (total * slope_ref[...]).astype(bf16)
    back = reorder(me_ref[0], tokens, order, back=True)
    pg_ref[...] = lax.dot_general(back, moved, (((1,), (1,)), ((), ())), preferred_element_type=f32).astype(bf16)
    results.append(pltpu.make_async_copy(pg_ref, pg_hbm, sems.at[len(parts)]))
    results[-1].start()
    for result in results:
        result.wait()


SMEM = functools.partial(pl.BlockSpec, memory_space=pltpu.SMEM)
VMEM = functools.partial(pl.BlockSpec, memory_space=pltpu.VMEM)
HBM = functools.partial(pl.BlockSpec, memory_space=pltpu.HBM)


def body(stream_sent, grad_sent, preact_now, preact_back, down_weight, block_mask):
    sections = lax.axis_size("section")
    stream, grad = stream_sent, grad_sent
    if sections > 1:
        section_index = lax.axis_index("section")
        stream = jnp.where(section_index == 0, stream, shifted(stream, "section", 1))
        grad = jnp.where(section_index == sections - 1, grad, shifted(grad, "section", -1))
    stream, grad, mask, weight = stream[0], grad[0], block_mask[0], down_weight[0]
    pre_now, pre_back = preact_now[0], preact_back[0]
    held = [pltpu.with_memory_space_constraint(x, pltpu.HBM) for x in (mask, pre_now, pre_back, weight)]
    tokens, hidden = preact_now.shape[1:]
    width = down_weight.shape[2]
    devices = lax.axis_size("blk")
    bits = [1 << k for k in range(devices.bit_length() - 1)]
    near, plane, far = bits[:1], bits[1:3], bits[3:]
    scatter_order = near + plane + far
    gather_order = near + plane + far[::-1]
    me = lax.axis_index("blk").astype(jnp.int32).reshape(1)
    half = tokens // 2

    def shape(dtype, *dims):
        return jax.ShapeDtypeStruct(dims, dtype)

    params = pltpu.CompilerParams(vmem_limit_bytes=LIMIT)
    total, send, masked, kept, held_back = pl.pallas_call(
        functools.partial(forward_kernel, scatter_order),
        out_shape=(
            shape(f32, half, width),
            shape(bf16, half, width),
            shape(bf16, hidden, width),
            shape(f32, hidden // BLOCK, width),
            shape(bf16, tokens, hidden),
        ),
        in_specs=[SMEM()] + [HBM()] * 4,
        out_specs=(VMEM(),) * 5,
        scratch_shapes=[
            pltpu.SMEM(mask.shape, jnp.int32),
            pltpu.VMEM((tokens, hidden), bf16),
            pltpu.VMEM((hidden, width), bf16),
            pltpu.SemaphoreType.DMA((3 + len(columns(width, WIDE)),)),
        ],
        compiler_params=params,
        cost_estimate=pl.CostEstimate(flops=2 * tokens * hidden * width, bytes_accessed=FORWARD_BYTES, transcendentals=0),
        name="forward",
    )(me, *held)

    hidden_back, slope = pl.pallas_call(
        functools.partial(prepare_kernel, gather_order),
        out_shape=(shape(bf16, hidden, tokens), shape(f32, hidden, tokens)),
        in_specs=[SMEM(), VMEM()],
        out_specs=(VMEM(),) * 2,
        compiler_params=params,
        cost_estimate=pl.CostEstimate(flops=2 * tokens * tokens * hidden, bytes_accessed=PREPARE_BYTES, transcendentals=0),
        name="prepare",
    )(me, held_back)

    mine = grad
    for k, bit in enumerate(far):
        other = exchange(mine, bit)
        if k == 0:
            send, other = lax.optimization_barrier((send, other))
        mine = jnp.concatenate([mine, other], axis=0)

    total = total + exchange(send, near[0]).astype(f32)
    parts = jnp.split(total, 1 << len(plane), axis=0)
    total = parts[0]
    for k in [2, 1, 3]:
        total = total + exchange(parts[k].astype(bf16), combinations(plane)[k]).astype(f32)
    for bit in far:
        part = total[total.shape[0] // 2 :].astype(bf16)
        total = total[: total.shape[0] // 2]
        if bit == far[-1]:
            total = total + stream.astype(f32)
        total = total + exchange(part, bit).astype(f32)
    stream_out = total.astype(bf16)

    masks = combinations(plane)
    places = [0] + [1, 3, 2]
    grads = [mine] + [exchange(mine, masks[k]) for k in places[1:]]
    mine = pl.pallas_call(
        functools.partial(pack_kernel, places),
        out_shape=shape(bf16, half, width),
        in_specs=[VMEM()] * len(grads),
        out_specs=VMEM(),
        compiler_params=params,
        name="pack",
    )(*grads)
    grads = [mine, exchange(mine, near[0])]

    weight_grad, preact_grad = pl.pallas_call(
        functools.partial(backward_kernel, gather_order, len(grads)),
        out_shape=(shape(bf16, hidden, width), shape(bf16, tokens, hidden)),
        in_specs=[SMEM()] + [VMEM()] * (len(grads) + 4),
        out_specs=(HBM(), HBM()),
        scratch_shapes=[
            pltpu.VMEM((tokens, width), bf16),
            pltpu.VMEM((hidden, width), bf16),
            pltpu.VMEM((tokens, hidden), bf16),
            pltpu.SemaphoreType.DMA((1 + len(columns(width, CHUNK)),)),
        ],
        compiler_params=params,
        cost_estimate=pl.CostEstimate(flops=4 * tokens * hidden * width, bytes_accessed=4 * hidden * width, transcendentals=0),
        name="backward",
    )(me, *grads, kept, masked, hidden_back, slope)
    return stream_out[None], preact_grad[None], weight_grad[None]


def solution(mesh):
    placed = (
        P("section", "blk", None),
        P("section", "blk", None),
        P("section", None, "blk"),
        P("section", None, "blk"),
        P("section", "blk", None),
        P("section", "blk", None),
    )
    return jax.shard_map(
        body,
        mesh=mesh,
        in_specs=placed,
        out_specs=(P("section", "blk", None), P("section", None, "blk"), P("section", "blk", None)),
        check_vma=False,
    )
```

```python
import functools
import math

import jax
import jax.numpy as jnp
from jax import lax
from jax.experimental import pallas as pl
from jax.experimental.pallas import tpu as pltpu
from jax.sharding import PartitionSpec as P

BLOCK = 128
SCALE = math.sqrt(2.0 / math.pi)
CUBIC = 0.044715
CHUNK = 768
WIDE = 1024
LIMIT = 16 * 1024 * 1024
FORWARD_BYTES = 6_000_000
PREPARE_BYTES = 1_500_000
bf16 = jnp.bfloat16
f32 = jnp.float32


def shifted(block, axis, distance):
    devices = range(lax.axis_size(axis))
    route = [(i - distance, i) for i in devices if i - distance in devices]
    return lax.ppermute(block, axis, route)


def exchange(block, bit):
    return lax.ppermute(block, "blk", [(i, i ^ bit) for i in range(lax.axis_size("blk"))])


def combinations(bits):
    found = [0]
    for bit in bits[::-1]:
        found += [bit ^ other for other in found]
    return found


def own_token(place, me, order, each):
    group, within = place // each, place % each
    owner = me
    for k, bit in enumerate(order):
        owner = owner ^ jnp.where((group >> (len(order) - 1 - k)) & 1 == 1, bit, 0)
    return owner * each + within


def reorder(me, tokens, order, back=False):
    rows = lax.broadcasted_iota(jnp.int32, (tokens, tokens), 1 if back else 0)
    cols = lax.broadcasted_iota(jnp.int32, (tokens, tokens), 0 if back else 1)
    return (own_token(rows, me, order, tokens >> len(order)) == cols).astype(bf16)


def columns(width, chunk):
    chunk = chunk if width % chunk == 0 else BLOCK
    return [pl.ds(first, chunk) for first in range(0, width, chunk)]


def keep_blocks(array, mask_ref, i, first):
    blocks = []
    for j in range(array.shape[1] // BLOCK):
        block = array[:, j * BLOCK : (j + 1) * BLOCK]
        blocks.append(jnp.where(mask_ref[i, first + j] != 0, block, jnp.zeros_like(block)))
    return jnp.concatenate(blocks, axis=1)


def gelu_and_slope(x):
    square = x * x
    t = jnp.tanh(SCALE * (x + CUBIC * x * square))
    half = 0.5 * (1.0 + t)
    slope = half + 0.5 * x * (1.0 - t * t) * (SCALE * (1.0 + 3.0 * CUBIC * square))
    return x * half, slope


def forward_kernel(order, me_ref, mask_hbm, now_hbm, back_hbm, w_hbm, *refs):
    total_ref, send_ref, masked_ref, kept_ref, back_ref, mask_ref, now_ref, w_ref, sems = refs
    parts = columns(w_ref.shape[1], WIDE)
    pairs = [(now_hbm, now_ref), (mask_hbm, mask_ref)]
    pairs += [(w_hbm.at[:, part], w_ref.at[:, part]) for part in parts]
    pairs += [(back_hbm, back_ref)]
    copies = [pltpu.make_async_copy(source, target, sems.at[k]) for k, (source, target) in enumerate(pairs)]
    for copy in copies:
        copy.start()
    tokens = now_ref.shape[0]
    half = send_ref.shape[0]
    moves = reorder(me_ref[0], tokens, order)
    copies[0].wait()
    hidden = gelu_and_slope(jnp.dot(moves, now_ref[...], preferred_element_type=f32))[0].astype(bf16)
    copies[1].wait()
    for i in range(w_ref.shape[0] // BLOCK):
        for j in range(w_ref.shape[1] // BLOCK):
            kept_ref[i : i + 1, j * BLOCK : (j + 1) * BLOCK] = jnp.where(mask_ref[i, j] != 0, jnp.ones((1, BLOCK), f32), 0.0)
    for c, part in enumerate(parts):
        copies[2 + c].wait()
        for i in range(w_ref.shape[0] // BLOCK):
            rows = pl.ds(i * BLOCK, BLOCK)
            masked_ref[rows, part] = keep_blocks(w_ref[rows, part], mask_ref, i, part.start // BLOCK)
        product = jnp.dot(hidden, masked_ref[:, part], preferred_element_type=f32)
        total_ref[:, part] = product[:half]
        send_ref[:, part] = product[half:].astype(bf16)
    copies[-1].wait()


def prepare_kernel(order, me_ref, back_ref, hidden_ref, slope_ref):
    moves = reorder(me_ref[0], back_ref.shape[0], order, back=True)
    hidden, slope = gelu_and_slope(jnp.dot(back_ref[...].T, moves, preferred_element_type=f32))
    hidden_ref[...] = hidden.astype(bf16)
    slope_ref[...] = slope


def pack_kernel(places, *refs):
    *pieces, out_ref = refs
    for k, piece in zip(places, pieces):
        rows = piece.shape[0]
        out_ref[k * rows : (k + 1) * rows] = piece[...]


def backward_kernel(order, pieces, me_ref, *refs):
    grads = refs[:pieces]
    kept_ref, w_ref, hidden_ref, slope_ref, wg_hbm, pg_hbm, grad_ref, wg_ref, pg_ref, sems = refs[pieces:]
    tokens = pg_ref.shape[0]
    parts = columns(w_ref.shape[1], CHUNK)
    results = []
    for c, part in enumerate(parts):
        for k, piece in enumerate(grads):
            rows = piece.shape[0]
            grad_ref[k * rows : (k + 1) * rows, part] = piece[:, part]
        full = jnp.dot(hidden_ref[...], grad_ref[:, part], preferred_element_type=f32)
        for i in range(w_ref.shape[0] // BLOCK):
            band = full[i * BLOCK : (i + 1) * BLOCK] * kept_ref[i : i + 1, part]
            wg_ref[pl.ds(i * BLOCK, BLOCK), part] = band.astype(bf16)
        results.append(pltpu.make_async_copy(wg_ref.at[:, part], wg_hbm.at[:, part], sems.at[c]))
        results[-1].start()
    total = jnp.zeros((w_ref.shape[0], tokens), f32)
    for part in parts:
        total += jnp.dot(w_ref[:, part], grad_ref[:, part].T, preferred_element_type=f32)
    moved = (total * slope_ref[...]).astype(bf16)
    back = reorder(me_ref[0], tokens, order, back=True)
    pg_ref[...] = lax.dot_general(back, moved, (((1,), (1,)), ((), ())), preferred_element_type=f32).astype(bf16)
    results.append(pltpu.make_async_copy(pg_ref, pg_hbm, sems.at[len(parts)]))
    results[-1].start()
    for result in results:
        result.wait()


SMEM = functools.partial(pl.BlockSpec, memory_space=pltpu.SMEM)
VMEM = functools.partial(pl.BlockSpec, memory_space=pltpu.VMEM)
HBM = functools.partial(pl.BlockSpec, memory_space=pltpu.HBM)


def body(stream_sent, grad_sent, preact_now, preact_back, down_weight, block_mask):
    sections = lax.axis_size("section")
    stream, grad = stream_sent, grad_sent
    if sections > 1:
        section_index = lax.axis_index("section")
        stream = jnp.where(section_index == 0, stream, shifted(stream, "section", 1))
        grad = jnp.where(section_index == sections - 1, grad, shifted(grad, "section", -1))
    stream, grad, mask, weight = stream[0], grad[0], block_mask[0], down_weight[0]
    pre_now, pre_back = preact_now[0], preact_back[0]
    held = [pltpu.with_memory_space_constraint(x, pltpu.HBM) for x in (mask, pre_now, pre_back, weight)]
    tokens, hidden = preact_now.shape[1:]
    width = down_weight.shape[2]
    devices = lax.axis_size("blk")
    bits = [1 << k for k in range(devices.bit_length() - 1)]
    near, plane, far = bits[:1], bits[1:3], bits[3:]
    scatter_order = near + plane + far
    gather_order = near + plane + far[::-1]
    me = lax.axis_index("blk").astype(jnp.int32).reshape(1)
    half = tokens // 2

    def shape(dtype, *dims):
        return jax.ShapeDtypeStruct(dims, dtype)

    params = pltpu.CompilerParams(vmem_limit_bytes=LIMIT)
    total, send, masked, kept, held_back = pl.pallas_call(
        functools.partial(forward_kernel, scatter_order),
        out_shape=(
            shape(f32, half, width),
            shape(bf16, half, width),
            shape(bf16, hidden, width),
            shape(f32, hidden // BLOCK, width),
            shape(bf16, tokens, hidden),
        ),
        in_specs=[SMEM()] + [HBM()] * 4,
        out_specs=(VMEM(),) * 5,
        scratch_shapes=[
            pltpu.SMEM(mask.shape, jnp.int32),
            pltpu.VMEM((tokens, hidden), bf16),
            pltpu.VMEM((hidden, width), bf16),
            pltpu.SemaphoreType.DMA((3 + len(columns(width, WIDE)),)),
        ],
        compiler_params=params,
        cost_estimate=pl.CostEstimate(flops=2 * tokens * hidden * width, bytes_accessed=FORWARD_BYTES, transcendentals=0),
        name="forward",
    )(me, *held)

    hidden_back, slope = pl.pallas_call(
        functools.partial(prepare_kernel, gather_order),
        out_shape=(shape(bf16, hidden, tokens), shape(f32, hidden, tokens)),
        in_specs=[SMEM(), VMEM()],
        out_specs=(VMEM(),) * 2,
        compiler_params=params,
        cost_estimate=pl.CostEstimate(flops=2 * tokens * tokens * hidden, bytes_accessed=PREPARE_BYTES, transcendentals=0),
        name="prepare",
    )(me, held_back)

    mine = grad
    for k, bit in enumerate(far):
        other = exchange(mine, bit)
        if k == 0:
            send, other = lax.optimization_barrier((send, other))
        mine = jnp.concatenate([mine, other], axis=0)

    total = total + exchange(send, near[0]).astype(f32)
    parts = jnp.split(total, 1 << len(plane), axis=0)
    total = parts[0]
    for k in [2, 1, 3]:
        total = total + exchange(parts[k].astype(bf16), combinations(plane)[k]).astype(f32)
    for bit in far:
        part = total[total.shape[0] // 2 :].astype(bf16)
        total = total[: total.shape[0] // 2]
        if bit == far[-1]:
            total = total + stream.astype(f32)
        total = total + exchange(part, bit).astype(f32)
    stream_out = total.astype(bf16)

    masks = combinations(plane)
    places = [0] + [1, 3, 2]
    grads = [mine] + [exchange(mine, masks[k]) for k in places[1:]]
    mine = pl.pallas_call(
        functools.partial(pack_kernel, places),
        out_shape=shape(bf16, half, width),
        in_specs=[VMEM()] * len(grads),
        out_specs=VMEM(),
        compiler_params=params,
        name="pack",
    )(*grads)
    grads = [mine, exchange(mine, near[0])]

    weight_grad, preact_grad = pl.pallas_call(
        functools.partial(backward_kernel, gather_order, len(grads)),
        out_shape=(shape(bf16, hidden, width), shape(bf16, tokens, hidden)),
        in_specs=[SMEM()] + [VMEM()] * (len(grads) + 4),
        out_specs=(HBM(), HBM()),
        scratch_shapes=[
            pltpu.VMEM((tokens, width), bf16),
            pltpu.VMEM((hidden, width), bf16),
            pltpu.VMEM((tokens, hidden), bf16),
            pltpu.SemaphoreType.DMA((1 + len(columns(width, CHUNK)),)),
        ],
        compiler_params=params,
        cost_estimate=pl.CostEstimate(flops=4 * tokens * hidden * width, bytes_accessed=4 * hidden * width, transcendentals=0),
        name="backward",
    )(me, *grads, kept, masked, hidden_back, slope)
    return stream_out[None], preact_grad[None], weight_grad[None]


def solution(mesh):
    placed = (
        P("section", "blk", None),
        P("section", "blk", None),
        P("section", None, "blk"),
        P("section", None, "blk"),
        P("section", "blk", None),
        P("section", "blk", None),
    )
    return jax.shard_map(
        body,
        mesh=mesh,
        in_specs=placed,
        out_specs=(P("section", "blk", None), P("section", None, "blk"), P("section", "blk", None)),
        check_vma=False,
    )
```

```python
import functools
import math

import jax
import jax.numpy as jnp
from jax import lax
from jax.experimental import pallas as pl
from jax.experimental.pallas import tpu as pltpu
from jax.sharding import PartitionSpec as P

BLOCK = 128
SCALE = math.sqrt(2.0 / math.pi)
CUBIC = 0.044715
CHUNK = 512
WIDE = 1024
LIMIT = 16 * 1024 * 1024
FORWARD_BYTES = 6_000_000
PREPARE_BYTES = 1_500_000
bf16 = jnp.bfloat16
f32 = jnp.float32


def shifted(block, axis, distance):
    devices = range(lax.axis_size(axis))
    route = [(i - distance, i) for i in devices if i - distance in devices]
    return lax.ppermute(block, axis, route)


def exchange(block, bit):
    return lax.ppermute(block, "blk", [(i, i ^ bit) for i in range(lax.axis_size("blk"))])


def combinations(bits):
    found = [0]
    for bit in bits[::-1]:
        found += [bit ^ other for other in found]
    return found


def own_token(place, me, order, each):
    group, within = place // each, place % each
    owner = me
    for k, bit in enumerate(order):
        owner = owner ^ jnp.where((group >> (len(order) - 1 - k)) & 1 == 1, bit, 0)
    return owner * each + within


def reorder(me, tokens, order, back=False):
    rows = lax.broadcasted_iota(jnp.int32, (tokens, tokens), 1 if back else 0)
    cols = lax.broadcasted_iota(jnp.int32, (tokens, tokens), 0 if back else 1)
    return (own_token(rows, me, order, tokens >> len(order)) == cols).astype(bf16)


def columns(width, chunk):
    chunk = chunk if width % chunk == 0 else BLOCK
    return [pl.ds(first, chunk) for first in range(0, width, chunk)]


def keep_blocks(array, mask_ref, i, first):
    blocks = []
    for j in range(array.shape[1] // BLOCK):
        block = array[:, j * BLOCK : (j + 1) * BLOCK]
        blocks.append(jnp.where(mask_ref[i, first + j] != 0, block, jnp.zeros_like(block)))
    return jnp.concatenate(blocks, axis=1)


def gelu_and_slope(x):
    square = x * x
    t = jnp.tanh(SCALE * (x + CUBIC * x * square))
    half = 0.5 * (1.0 + t)
    slope = half + 0.5 * x * (1.0 - t * t) * (SCALE * (1.0 + 3.0 * CUBIC * square))
    return x * half, slope


def forward_kernel(order, me_ref, mask_hbm, now_hbm, back_hbm, w_hbm, *refs):
    total_ref, send_ref, masked_ref, kept_ref, back_ref, mask_ref, now_ref, w_ref, sems = refs
    parts = columns(w_ref.shape[1], WIDE)
    pairs = [(now_hbm, now_ref), (mask_hbm, mask_ref)]
    pairs += [(w_hbm.at[:, part], w_ref.at[:, part]) for part in parts]
    pairs += [(back_hbm, back_ref)]
    copies = [pltpu.make_async_copy(source, target, sems.at[k]) for k, (source, target) in enumerate(pairs)]
    for copy in copies:
        copy.start()
    tokens = now_ref.shape[0]
    half = send_ref.shape[0]
    moves = reorder(me_ref[0], tokens, order)
    copies[0].wait()
    hidden = gelu_and_slope(jnp.dot(moves, now_ref[...], preferred_element_type=f32))[0].astype(bf16)
    copies[1].wait()
    for i in range(w_ref.shape[0] // BLOCK):
        for j in range(w_ref.shape[1] // BLOCK):
            kept_ref[i : i + 1, j * BLOCK : (j + 1) * BLOCK] = jnp.where(mask_ref[i, j] != 0, jnp.ones((1, BLOCK), f32), 0.0)
    for c, part in enumerate(parts):
        copies[2 + c].wait()
        for i in range(w_ref.shape[0] // BLOCK):
            rows = pl.ds(i * BLOCK, BLOCK)
            masked_ref[rows, part] = keep_blocks(w_ref[rows, part], mask_ref, i, part.start // BLOCK)
        product = jnp.dot(hidden, masked_ref[:, part], preferred_element_type=f32)
        total_ref[:, part] = product[:half]
        send_ref[:, part] = product[half:].astype(bf16)
    copies[-1].wait()


def prepare_kernel(order, me_ref, back_ref, hidden_ref, slope_ref):
    moves = reorder(me_ref[0], back_ref.shape[0], order, back=True)
    hidden, slope = gelu_and_slope(jnp.dot(back_ref[...].T, moves, preferred_element_type=f32))
    hidden_ref[...] = hidden.astype(bf16)
    slope_ref[...] = slope


def pack_kernel(places, *refs):
    *pieces, out_ref = refs
    for k, piece in zip(places, pieces):
        rows = piece.shape[0]
        out_ref[k * rows : (k + 1) * rows] = piece[...]


def backward_kernel(order, pieces, me_ref, *refs):
    grads = refs[:pieces]
    kept_ref, w_ref, hidden_ref, slope_ref, wg_hbm, pg_hbm, grad_ref, wg_ref, pg_ref, sems = refs[pieces:]
    tokens = pg_ref.shape[0]
    parts = columns(w_ref.shape[1], CHUNK)
    results = []
    for c, part in enumerate(parts):
        for k, piece in enumerate(grads):
            rows = piece.shape[0]
            grad_ref[k * rows : (k + 1) * rows, part] = piece[:, part]
        full = jnp.dot(hidden_ref[...], grad_ref[:, part], preferred_element_type=f32)
        for i in range(w_ref.shape[0] // BLOCK):
            band = full[i * BLOCK : (i + 1) * BLOCK] * kept_ref[i : i + 1, part]
            wg_ref[pl.ds(i * BLOCK, BLOCK), part] = band.astype(bf16)
        results.append(pltpu.make_async_copy(wg_ref.at[:, part], wg_hbm.at[:, part], sems.at[c]))
        results[-1].start()
    total = lax.dot_general(w_ref[...], grad_ref[...], (((1,), (1,)), ((), ())), preferred_element_type=f32)
    moved = (total * slope_ref[...]).astype(bf16)
    back = reorder(me_ref[0], tokens, order, back=True)
    pg_ref[...] = lax.dot_general(back, moved, (((1,), (1,)), ((), ())), preferred_element_type=f32).astype(bf16)
    results.append(pltpu.make_async_copy(pg_ref, pg_hbm, sems.at[len(parts)]))
    results[-1].start()
    for result in results:
        result.wait()


SMEM = functools.partial(pl.BlockSpec, memory_space=pltpu.SMEM)
VMEM = functools.partial(pl.BlockSpec, memory_space=pltpu.VMEM)
HBM = functools.partial(pl.BlockSpec, memory_space=pltpu.HBM)


def body(stream_sent, grad_sent, preact_now, preact_back, down_weight, block_mask):
    sections = lax.axis_size("section")
    stream, grad = stream_sent, grad_sent
    if sections > 1:
        section_index = lax.axis_index("section")
        stream = jnp.where(section_index == 0, stream, shifted(stream, "section", 1))
        grad = jnp.where(section_index == sections - 1, grad, shifted(grad, "section", -1))
    stream, grad, mask, weight = stream[0], grad[0], block_mask[0], down_weight[0]
    pre_now, pre_back = preact_now[0], preact_back[0]
    held = [pltpu.with_memory_space_constraint(x, pltpu.HBM) for x in (mask, pre_now, pre_back, weight)]
    tokens, hidden = preact_now.shape[1:]
    width = down_weight.shape[2]
    devices = lax.axis_size("blk")
    bits = [1 << k for k in range(devices.bit_length() - 1)]
    near, plane, far = bits[:1], bits[1:3], bits[3:]
    scatter_order = near + plane + far
    gather_order = near + plane + far[::-1]
    me = lax.axis_index("blk").astype(jnp.int32).reshape(1)
    half = tokens // 2

    def shape(dtype, *dims):
        return jax.ShapeDtypeStruct(dims, dtype)

    params = pltpu.CompilerParams(vmem_limit_bytes=LIMIT)
    total, send, masked, kept, held_back = pl.pallas_call(
        functools.partial(forward_kernel, scatter_order),
        out_shape=(
            shape(f32, half, width),
            shape(bf16, half, width),
            shape(bf16, hidden, width),
            shape(f32, hidden // BLOCK, width),
            shape(bf16, tokens, hidden),
        ),
        in_specs=[SMEM()] + [HBM()] * 4,
        out_specs=(VMEM(),) * 5,
        scratch_shapes=[
            pltpu.SMEM(mask.shape, jnp.int32),
            pltpu.VMEM((tokens, hidden), bf16),
            pltpu.VMEM((hidden, width), bf16),
            pltpu.SemaphoreType.DMA((3 + len(columns(width, WIDE)),)),
        ],
        compiler_params=params,
        cost_estimate=pl.CostEstimate(flops=2 * tokens * hidden * width, bytes_accessed=FORWARD_BYTES, transcendentals=0),
        name="forward",
    )(me, *held)

    hidden_back, slope = pl.pallas_call(
        functools.partial(prepare_kernel, gather_order),
        out_shape=(shape(bf16, hidden, tokens), shape(f32, hidden, tokens)),
        in_specs=[SMEM(), VMEM()],
        out_specs=(VMEM(),) * 2,
        compiler_params=params,
        cost_estimate=pl.CostEstimate(flops=2 * tokens * tokens * hidden, bytes_accessed=PREPARE_BYTES, transcendentals=0),
        name="prepare",
    )(me, held_back)

    mine = grad
    for k, bit in enumerate(far):
        other = exchange(mine, bit)
        if k == 0:
            send, other = lax.optimization_barrier((send, other))
        mine = jnp.concatenate([mine, other], axis=0)

    total = total + exchange(send, near[0]).astype(f32)
    parts = jnp.split(total, 1 << len(plane), axis=0)
    total = parts[0]
    for k in [2, 1, 3]:
        total = total + exchange(parts[k].astype(bf16), combinations(plane)[k]).astype(f32)
    for bit in far:
        part = total[total.shape[0] // 2 :].astype(bf16)
        total = total[: total.shape[0] // 2]
        if bit == far[-1]:
            total = total + stream.astype(f32)
        total = total + exchange(part, bit).astype(f32)
    stream_out = total.astype(bf16)

    masks = combinations(plane)
    places = [0] + [2, 3, 1]
    grads = [mine] + [exchange(mine, masks[k]) for k in places[1:]]
    mine = pl.pallas_call(
        functools.partial(pack_kernel, places),
        out_shape=shape(bf16, half, width),
        in_specs=[VMEM()] * len(grads),
        out_specs=VMEM(),
        compiler_params=params,
        name="pack",
    )(*grads)
    grads = [mine, exchange(mine, near[0])]

    weight_grad, preact_grad = pl.pallas_call(
        functools.partial(backward_kernel, gather_order, len(grads)),
        out_shape=(shape(bf16, hidden, width), shape(bf16, tokens, hidden)),
        in_specs=[SMEM()] + [VMEM()] * (len(grads) + 4),
        out_specs=(HBM(), HBM()),
        scratch_shapes=[
            pltpu.VMEM((tokens, width), bf16),
            pltpu.VMEM((hidden, width), bf16),
            pltpu.VMEM((tokens, hidden), bf16),
            pltpu.SemaphoreType.DMA((1 + len(columns(width, CHUNK)),)),
        ],
        compiler_params=params,
        cost_estimate=pl.CostEstimate(flops=4 * tokens * hidden * width, bytes_accessed=4 * hidden * width, transcendentals=0),
        name="backward",
    )(me, *grads, kept, masked, hidden_back, slope)
    return stream_out[None], preact_grad[None], weight_grad[None]


def solution(mesh):
    placed = (
        P("section", "blk", None),
        P("section", "blk", None),
        P("section", None, "blk"),
        P("section", None, "blk"),
        P("section", "blk", None),
        P("section", "blk", None),
    )
    return jax.shard_map(
        body,
        mesh=mesh,
        in_specs=placed,
        out_specs=(P("section", "blk", None), P("section", None, "blk"), P("section", "blk", None)),
        check_vma=False,
    )
```

```python
import functools
import math

import jax
import jax.numpy as jnp
from jax import lax
from jax.experimental import pallas as pl
from jax.experimental.pallas import tpu as pltpu
from jax.sharding import PartitionSpec as P

BLOCK = 128
SCALE = math.sqrt(2.0 / math.pi)
CUBIC = 0.044715
CHUNK = 512
WIDE = 1024
LIMIT = 16 * 1024 * 1024
FORWARD_BYTES = 6_000_000
PREPARE_BYTES = 1_500_000
bf16 = jnp.bfloat16
f32 = jnp.float32


def shifted(block, axis, distance):
    devices = range(lax.axis_size(axis))
    route = [(i - distance, i) for i in devices if i - distance in devices]
    return lax.ppermute(block, axis, route)


def exchange(block, bit):
    return lax.ppermute(block, "blk", [(i, i ^ bit) for i in range(lax.axis_size("blk"))])


def combinations(bits):
    found = [0]
    for bit in bits[::-1]:
        found += [bit ^ other for other in found]
    return found


def own_token(place, me, order, each):
    group, within = place // each, place % each
    owner = me
    for k, bit in enumerate(order):
        owner = owner ^ jnp.where((group >> (len(order) - 1 - k)) & 1 == 1, bit, 0)
    return owner * each + within


def reorder(me, tokens, order, back=False):
    rows = lax.broadcasted_iota(jnp.int32, (tokens, tokens), 1 if back else 0)
    cols = lax.broadcasted_iota(jnp.int32, (tokens, tokens), 0 if back else 1)
    return (own_token(rows, me, order, tokens >> len(order)) == cols).astype(bf16)


def columns(width, chunk):
    chunk = chunk if width % chunk == 0 else BLOCK
    return [pl.ds(first, chunk) for first in range(0, width, chunk)]


def keep_blocks(array, mask_ref, i, first):
    blocks = []
    for j in range(array.shape[1] // BLOCK):
        block = array[:, j * BLOCK : (j + 1) * BLOCK]
        blocks.append(jnp.where(mask_ref[i, first + j] != 0, block, jnp.zeros_like(block)))
    return jnp.concatenate(blocks, axis=1)


def gelu_and_slope(x):
    square = x * x
    t = jnp.tanh(SCALE * (x + CUBIC * x * square))
    half = 0.5 * (1.0 + t)
    slope = half + 0.5 * x * (1.0 - t * t) * (SCALE * (1.0 + 3.0 * CUBIC * square))
    return x * half, slope


def forward_kernel(order, me_ref, mask_hbm, now_hbm, back_hbm, w_hbm, *refs):
    total_ref, send_ref, masked_ref, kept_ref, back_ref, mask_ref, now_ref, w_ref, sems = refs
    parts = columns(w_ref.shape[1], WIDE)
    pairs = [(now_hbm, now_ref), (mask_hbm, mask_ref)]
    pairs += [(w_hbm.at[:, part], w_ref.at[:, part]) for part in parts]
    pairs += [(back_hbm, back_ref)]
    copies = [pltpu.make_async_copy(source, target, sems.at[k]) for k, (source, target) in enumerate(pairs)]
    for copy in copies:
        copy.start()
    tokens = now_ref.shape[0]
    half = send_ref.shape[0]
    moves = reorder(me_ref[0], tokens, order)
    copies[0].wait()
    hidden = gelu_and_slope(jnp.dot(moves, now_ref[...], preferred_element_type=f32))[0].astype(bf16)
    copies[1].wait()
    for i in range(w_ref.shape[0] // BLOCK):
        for j in range(w_ref.shape[1] // BLOCK):
            kept_ref[i : i + 1, j * BLOCK : (j + 1) * BLOCK] = jnp.where(mask_ref[i, j] != 0, jnp.ones((1, BLOCK), f32), 0.0)
    for c, part in enumerate(parts):
        copies[2 + c].wait()
        for i in range(w_ref.shape[0] // BLOCK):
            rows = pl.ds(i * BLOCK, BLOCK)
            masked_ref[rows, part] = keep_blocks(w_ref[rows, part], mask_ref, i, part.start // BLOCK)
        product = jnp.dot(hidden, masked_ref[:, part], preferred_element_type=f32)
        total_ref[:, part] = product[:half]
        send_ref[:, part] = product[half:].astype(bf16)
    copies[-1].wait()


def prepare_kernel(order, me_ref, back_ref, hidden_ref, slope_ref):
    moves = reorder(me_ref[0], back_ref.shape[0], order, back=True)
    hidden, slope = gelu_and_slope(jnp.dot(back_ref[...].T, moves, preferred_element_type=f32))
    hidden_ref[...] = hidden.astype(bf16)
    slope_ref[...] = slope


def pack_kernel(places, *refs):
    *pieces, out_ref = refs
    for k, piece in zip(places, pieces):
        rows = piece.shape[0]
        out_ref[k * rows : (k + 1) * rows] = piece[...]


def backward_kernel(order, pieces, me_ref, *refs):
    grads = refs[:pieces]
    kept_ref, w_ref, hidden_ref, slope_ref, wg_hbm, pg_hbm, grad_ref, wg_ref, pg_ref, sems = refs[pieces:]
    tokens = pg_ref.shape[0]
    parts = columns(w_ref.shape[1], CHUNK)
    results = []
    for c, part in enumerate(parts):
        for k, piece in enumerate(grads):
            rows = piece.shape[0]
            grad_ref[k * rows : (k + 1) * rows, part] = piece[:, part]
        full = jnp.dot(hidden_ref[...], grad_ref[:, part], preferred_element_type=f32)
        for i in range(w_ref.shape[0] // BLOCK):
            band = full[i * BLOCK : (i + 1) * BLOCK] * kept_ref[i : i + 1, part]
            wg_ref[pl.ds(i * BLOCK, BLOCK), part] = band.astype(bf16)
        results.append(pltpu.make_async_copy(wg_ref.at[:, part], wg_hbm.at[:, part], sems.at[c]))
        results[-1].start()
    total = jnp.zeros((w_ref.shape[0], tokens), f32)
    for part in parts:
        total += jnp.dot(w_ref[:, part], grad_ref[:, part].T, preferred_element_type=f32)
    moved = (total * slope_ref[...]).astype(bf16)
    back = reorder(me_ref[0], tokens, order, back=True)
    pg_ref[...] = lax.dot_general(back, moved, (((1,), (1,)), ((), ())), preferred_element_type=f32).astype(bf16)
    results.append(pltpu.make_async_copy(pg_ref, pg_hbm, sems.at[len(parts)]))
    results[-1].start()
    for result in results:
        result.wait()


SMEM = functools.partial(pl.BlockSpec, memory_space=pltpu.SMEM)
VMEM = functools.partial(pl.BlockSpec, memory_space=pltpu.VMEM)
HBM = functools.partial(pl.BlockSpec, memory_space=pltpu.HBM)


def body(stream_sent, grad_sent, preact_now, preact_back, down_weight, block_mask):
    sections = lax.axis_size("section")
    stream, grad = stream_sent, grad_sent
    if sections > 1:
        section_index = lax.axis_index("section")
        stream = jnp.where(section_index == 0, stream, shifted(stream, "section", 1))
        grad = jnp.where(section_index == sections - 1, grad, shifted(grad, "section", -1))
    stream, grad, mask, weight = stream[0], grad[0], block_mask[0], down_weight[0]
    pre_now, pre_back = preact_now[0], preact_back[0]
    held = [pltpu.with_memory_space_constraint(x, pltpu.HBM) for x in (mask, pre_now, pre_back, weight)]
    tokens, hidden = preact_now.shape[1:]
    width = down_weight.shape[2]
    devices = lax.axis_size("blk")
    bits = [1 << k for k in range(devices.bit_length() - 1)]
    near, plane, far = bits[:1], bits[1:3], bits[3:]
    scatter_order = near + plane + far
    gather_order = near + plane + far[::-1]
    me = lax.axis_index("blk").astype(jnp.int32).reshape(1)
    half = tokens // 2

    def shape(dtype, *dims):
        return jax.ShapeDtypeStruct(dims, dtype)

    params = pltpu.CompilerParams(vmem_limit_bytes=LIMIT)
    total, send, masked, kept, held_back = pl.pallas_call(
        functools.partial(forward_kernel, scatter_order),
        out_shape=(
            shape(f32, half, width),
            shape(bf16, half, width),
            shape(bf16, hidden, width),
            shape(f32, hidden // BLOCK, width),
            shape(bf16, tokens, hidden),
        ),
        in_specs=[SMEM()] + [HBM()] * 4,
        out_specs=(VMEM(),) * 5,
        scratch_shapes=[
            pltpu.SMEM(mask.shape, jnp.int32),
            pltpu.VMEM((tokens, hidden), bf16),
            pltpu.VMEM((hidden, width), bf16),
            pltpu.SemaphoreType.DMA((3 + len(columns(width, WIDE)),)),
        ],
        compiler_params=params,
        cost_estimate=pl.CostEstimate(flops=2 * tokens * hidden * width, bytes_accessed=FORWARD_BYTES, transcendentals=0),
        name="forward",
    )(me, *held)

    hidden_back, slope = pl.pallas_call(
        functools.partial(prepare_kernel, gather_order),
        out_shape=(shape(bf16, hidden, tokens), shape(f32, hidden, tokens)),
        in_specs=[SMEM(), VMEM()],
        out_specs=(VMEM(),) * 2,
        compiler_params=params,
        cost_estimate=pl.CostEstimate(flops=2 * tokens * tokens * hidden, bytes_accessed=PREPARE_BYTES, transcendentals=0),
        name="prepare",
    )(me, held_back)

    mine = grad
    for k, bit in enumerate(far):
        other = exchange(mine, bit)
        if k == 0:
            send, other = lax.optimization_barrier((send, other))
        mine = jnp.concatenate([mine, other], axis=0)

    total = total + exchange(send, near[0]).astype(f32)
    parts = jnp.split(total, 1 << len(plane), axis=0)
    total = parts[0]
    for k in [2, 1, 3]:
        total = total + exchange(parts[k].astype(bf16), combinations(plane)[k]).astype(f32)
    for bit in far:
        part = total[total.shape[0] // 2 :].astype(bf16)
        total = total[: total.shape[0] // 2]
        if bit == far[-1]:
            total = total + stream.astype(f32)
        total = total + exchange(part, bit).astype(f32)
    stream_out = total.astype(bf16)

    masks = combinations(plane)
    places = [0] + [2, 3, 1]
    grads = [mine] + [exchange(mine, masks[k]) for k in places[1:]]
    mine = pl.pallas_call(
        functools.partial(pack_kernel, places),
        out_shape=shape(bf16, half, width),
        in_specs=[VMEM()] * len(grads),
        out_specs=VMEM(),
        compiler_params=params,
        name="pack",
    )(*grads)
    grads = [mine, exchange(mine, near[0])]

    weight_grad, preact_grad = pl.pallas_call(
        functools.partial(backward_kernel, gather_order, len(grads)),
        out_shape=(shape(bf16, hidden, width), shape(bf16, tokens, hidden)),
        in_specs=[SMEM()] + [VMEM()] * (len(grads) + 4),
        out_specs=(HBM(), HBM()),
        scratch_shapes=[
            pltpu.VMEM((tokens, width), bf16),
            pltpu.VMEM((hidden, width), bf16),
            pltpu.VMEM((tokens, hidden), bf16),
            pltpu.SemaphoreType.DMA((1 + len(columns(width, CHUNK)),)),
        ],
        compiler_params=params,
        cost_estimate=pl.CostEstimate(flops=4 * tokens * hidden * width, bytes_accessed=4 * hidden * width, transcendentals=0),
        name="backward",
    )(me, *grads, kept, masked, hidden_back, slope)
    return stream_out[None], preact_grad[None], weight_grad[None]


def solution(mesh):
    placed = (
        P("section", "blk", None),
        P("section", "blk", None),
        P("section", None, "blk"),
        P("section", None, "blk"),
        P("section", "blk", None),
        P("section", "blk", None),
    )
    return jax.shard_map(
        body,
        mesh=mesh,
        in_specs=placed,
        out_specs=(P("section", "blk", None), P("section", None, "blk"), P("section", "blk", None)),
        check_vma=False,
    )
```
